256 devices in a mesh: pipe: 2 (over core), expert: 32 (over z, x), dp: 4 (over y).
Axes of the slice: x: 4, y: 4, z: 8, core: 2. Of those that a mesh axis runs over, the one named last changes fastest.
Arguments:
- layer_input: bfloat16 [2, 16384, 4096], P('pipe', ('expert', 'dp')), may hold values from -6 to 6
- out_grad: bfloat16 [2, 16384, 4096], P('pipe', ('expert', 'dp')), may hold values from -2 to 2
- routes: int32 [2, 16384, 1], P('pipe', ('expert', 'dp')), may hold values from 0 to 15; in each aligned block of 128 rows (0 to 127, 128 to 255, ..., all dimensions but the last counted through in order) at most 16 rows name the same one
- gates: float32 [2, 16384], P('pipe', ('expert', 'dp')), may hold values from 0.2 to 1
- w_gate: bfloat16 [2, 4096, 12288], P('pipe', 'dp', 'expert'), may hold values from -0.09375 to 0.09375
- w_up: bfloat16 [2, 4096, 12288], P('pipe', 'dp', 'expert'), may hold values from -0.09375 to 0.09375
- w_down: bfloat16 [2, 4096, 12288], P('pipe', 'dp', 'expert'), may hold values from -0.21875 to 0.21875
Outputs:
- passed_grad: bfloat16 [2, 16384, 4096], P('pipe', ('expert', 'dp'))
- grad_gate: float32 [2, 4096, 12288], P('pipe', 'dp', 'expert')
- grad_up: float32 [2, 4096, 12288], P('pipe', 'dp', 'expert')
- grad_down: float32 [2, 4096, 12288], P('pipe', 'dp', 'expert')
The draws below stay inside these ranges and needn't reach their ends.
Inputs may be any that keep to these rules, and one draw needn't show every extreme that they name: `routes`: among the 128 tokens of one device, at most 16 have the same expert.
All inputs are finite; a program needn't handle non-finite values.
Results may differ from the reference program's by a relative error of at most 0.012.
Values may be sent and summed in bfloat16 or wider, within the bound.
No kernel may reach another device: no remote copies, remote signals or barrier semaphores. Data moves between devices by JAX's collectives and lax.ppermute only.
A program may use at most 128 MiB of HBM per device.

```python
import math
import jax
import jax.numpy as jnp
import numpy as np
from jax import lax

D = 4096
HID = 768
SHARDS = 2
TOK_DEV = 128
HALF = 384
EXPERTS = 16
CAP = 16
SECTIONS = 2
TOKENS = 16384
N_EXPERT = 32
N_DP = 4


def block_scale(own_key, extent, shards, least, high):
    def one(axis_at, shards_of):
        draws = jax.random.uniform(jax.random.fold_in(jax.random.fold_in(own_key, 6), axis_at), (shards_of,), jnp.float32, least / len(shards), high / len(shards))
        return jnp.repeat(jnp.exp(draws), extent[axis_at] // shards_of).reshape((-1,) + (1,) * (len(extent) - axis_at - 1))

    level = one(*shards[0])
    for cut in shards[1:]:
        level = level * one(*cut)
    return level


def shared_out(rng, own, number, rows, count, top, bound, skew):
    ranking = jax.random.permutation(rng, count)
    crowded, usual = load_shares(count, rows * top, bound, skew, True), load_shares(count, rows * top, bound, skew, False)
    places = jnp.arange(count)

    def named(lengths, turn):
        used = int((lengths > 0).sum())
        fixed = max(1, used // 4)
        shifted = fixed + (places - fixed + turn * (used - fixed)) % max(1, count - fixed)
        return jnp.zeros((count,), jnp.int32).at[ranking[jnp.where(places < fixed, places, shifted)]].set(jnp.asarray(lengths, jnp.int32))

    lengths = jnp.where(number % 4 == 0, named(crowded, number // 4), named(usual, number - number // 4 - 1))
    mixed = jax.random.permutation(jax.random.fold_in(own, 3), count)
    donor, taker = mixed[0:count // 2 * 2:2], mixed[1:count // 2 * 2:2]
    slack = jnp.minimum(lengths[donor] - 1, bound - lengths[taker]) // 2
    slack = jnp.where((donor == ranking[0]) | (taker == ranking[0]) | (lengths[taker] == 0), 0, jnp.maximum(slack, 0))
    shifted = jax.random.randint(jax.random.fold_in(own, 4), (count // 2,), 0, 1 << 20) % (slack + 1)
    lengths = lengths.at[donor].add(-shifted).at[taker].add(shifted)
    labels = jnp.searchsorted(jnp.cumsum(lengths), jnp.arange(rows * top), side="right").astype(jnp.int32)
    listing = labels.reshape(top, rows).T
    listing = listing[jax.random.permutation(jax.random.fold_in(own, 1), rows)]
    turn = jax.random.randint(jax.random.fold_in(own, 2), (rows, 1), 0, top)
    return jnp.take_along_axis(listing, (jnp.arange(top)[None, :] + turn) % top, axis=1)


def load_shares(number_of, total, bound, skew, full):
    loads = [(1 << 20) // math.isqrt(grade ** skew) + 1 for grade in range(1, number_of + 1)]
    largest = bound if full else min(bound, max(-(-total // number_of), total * loads[0] // sum(loads)))
    least = 1 if total - largest >= number_of - 1 else 0
    given, surplus = [largest] + [least] * (number_of - 1), total - largest - least * (number_of - 1)
    while surplus > 0:
        movable = [i for i in range(1, number_of) if given[i] < largest] or [i for i in range(1, number_of) if given[i] < bound]
        pool, budget = sum([loads[i] for i in movable]), surplus
        for i in movable:
            more = min(bound - given[i], max(1, budget * loads[i] // pool), surplus)
            given[i] = given[i] + more
            surplus = surplus - more
    return np.array(given)


def gaussian(key, extent, deviation, reach, split=(), kind=jnp.bfloat16):
    factor_of = block_scale(key, extent, split, -0.22, 0.18) if split else 1.0
    drawn = jax.random.normal(key, extent, jnp.float32) * deviation * factor_of
    return jnp.minimum(jnp.maximum(drawn, -reach), reach).astype(kind)


def setup_inputs(seed: int = 0) -> dict:
    arg_keys = jax.random.split(jax.random.key(seed), 8)
    layer_input = gaussian(arg_keys[0], (SECTIONS, TOKENS, D), 1.0, 6.0, ((0, 2), (1, 128)))
    out_grad = gaussian(arg_keys[1], (SECTIONS, TOKENS, D), 0.25, 2.0, ((0, 2), (1, 128)))
    routes_keys = jax.random.split(jax.random.fold_in(arg_keys[2], 1), SECTIONS * TOKENS // TOK_DEV)
    routes_turns = jax.random.permutation(jax.random.fold_in(arg_keys[2], 3), SECTIONS * TOKENS // TOK_DEV)
    routes = jax.vmap(lambda own, number: shared_out(jax.random.fold_in(arg_keys[2], 2), own, number, TOK_DEV, EXPERTS, 1, CAP, 2))(routes_keys, routes_turns).reshape((SECTIONS, TOKENS, 1))
    gates = jnp.clip(0.2 + 0.8 * jax.random.uniform(arg_keys[3], (SECTIONS, TOKENS), jnp.float32) ** block_scale(arg_keys[3], (SECTIONS, TOKENS), ((0, 2), (1, 128)), -0.2, 0.2), 0.2, 1.0)
    w_gate = gaussian(arg_keys[4], (SECTIONS, D, EXPERTS * HID), D ** -0.5, 0.09375, ((0, 2), (1, 4), (2, 32)))
    w_up = gaussian(arg_keys[5], (SECTIONS, D, EXPERTS * HID), D ** -0.5, 0.09375, ((0, 2), (1, 4), (2, 32)))
    w_down = gaussian(arg_keys[6], (SECTIONS, D, EXPERTS * HID), HID ** -0.5, 0.21875, ((0, 2), (1, 4), (2, 32)))
    return dict(layer_input=layer_input, out_grad=out_grad, routes=routes, gates=gates, w_gate=w_gate, w_up=w_up, w_down=w_down)


def expert_math(x_rows, dy_rows, gate_cols, up_cols, down_cols):
    gate_pre = jnp.dot(x_rows, gate_cols, preferred_element_type=jnp.float32)
    up_pre = jnp.dot(x_rows, up_cols, preferred_element_type=jnp.float32)
    sigmoid_gate = jax.nn.sigmoid(gate_pre)
    silu_gate = gate_pre * sigmoid_gate
    hidden = (silu_gate * up_pre).astype(jnp.bfloat16)
    d_hidden = jnp.dot(dy_rows, down_cols, preferred_element_type=jnp.float32)
    d_up = (d_hidden * silu_gate).astype(jnp.bfloat16)
    d_gate = (d_hidden * up_pre * sigmoid_gate * (1.0 + gate_pre * (1.0 - sigmoid_gate))).astype(jnp.bfloat16)
    return hidden, d_gate, d_up


def back_rows(d_gate, d_up, gate_cols, up_cols):
    inner = (((1,), (1,)), ((), ()))
    first = lax.dot_general(d_gate, gate_cols, inner, preferred_element_type=jnp.float32)
    return first + lax.dot_general(d_up, up_cols, inner, preferred_element_type=jnp.float32)


def rounded(value):
    return lax.optimization_barrier(value.astype(jnp.bfloat16)).astype(jnp.float32)


def section_math(tokens, grads, route, weight, gate_all, up_all, down_all):
    outer = (((0,), (0,)), ((), ()))
    scaled = (weight[:, None] * grads.astype(jnp.float32)).astype(jnp.bfloat16)
    group = (jnp.arange(TOKENS, dtype=jnp.int32) // TOK_DEV) % N_DP
    sort_key = group * EXPERTS + route
    order = jnp.argsort(sort_key, stable=True).astype(jnp.int32)
    counts = jnp.sum((sort_key[:, None] == jnp.arange(N_DP * EXPERTS, dtype=jnp.int32)[None, :]).astype(jnp.int32), axis=0)
    starts = (jnp.cumsum(counts) - counts).astype(jnp.int32)
    segment = N_EXPERT * CAP
    padding = jnp.zeros((segment, D), jnp.bfloat16)
    sorted_x = jnp.concatenate([tokens[order], padding], axis=0)
    sorted_dy = jnp.concatenate([scaled[order], padding], axis=0)
    where_to = jnp.concatenate([order, jnp.full((segment,), TOKENS, jnp.int32)], axis=0)

    def one_expert(carry, expert):
        start_col = (expert * HID).astype(jnp.int32)
        gate_cols = lax.dynamic_slice_in_dim(gate_all, start_col, HID, 1)
        up_cols = lax.dynamic_slice_in_dim(up_all, start_col, HID, 1)
        down_cols = lax.dynamic_slice_in_dim(down_all, start_col, HID, 1)
        total_gate = jnp.zeros((D, HID), jnp.float32)
        total_up = jnp.zeros((D, HID), jnp.float32)
        total_down = jnp.zeros((D, HID), jnp.float32)
        for group_index in range(N_DP):
            slot_key = group_index * EXPERTS + expert
            first_row = starts[slot_key]
            live = jnp.arange(segment, dtype=jnp.int32) < counts[slot_key]
            x_rows = jnp.where(live[:, None], lax.dynamic_slice_in_dim(sorted_x, first_row, segment, 0), jnp.zeros((), jnp.bfloat16))
            dy_rows = jnp.where(live[:, None], lax.dynamic_slice_in_dim(sorted_dy, first_row, segment, 0), jnp.zeros((), jnp.bfloat16))
            targets = jnp.where(live, lax.dynamic_slice_in_dim(where_to, first_row, segment, 0), TOKENS).astype(jnp.int32)
            hidden, d_gate, d_up = expert_math(x_rows, dy_rows, gate_cols, up_cols, down_cols)
            row_sum = jnp.zeros((segment, D), jnp.float32)
            for half_index in range(SHARDS):
                low = half_index * HALF
                part = back_rows(d_gate[:, low:low + HALF], d_up[:, low:low + HALF], gate_cols[:, low:low + HALF], up_cols[:, low:low + HALF])
                row_sum = row_sum + part.astype(jnp.bfloat16).astype(jnp.float32)
            carry = carry.at[targets].set(row_sum.astype(jnp.bfloat16))
            total_gate = total_gate + rounded(lax.dot_general(x_rows, d_gate, outer, preferred_element_type=jnp.float32))
            total_up = total_up + rounded(lax.dot_general(x_rows, d_up, outer, preferred_element_type=jnp.float32))
            total_down = total_down + rounded(lax.dot_general(dy_rows, hidden, outer, preferred_element_type=jnp.float32))
        return carry, (total_gate, total_up, total_down)

    start_carry = jnp.zeros((TOKENS + 1, D), jnp.bfloat16)
    final, stacked = lax.scan(one_expert, start_carry, jnp.arange(EXPERTS, dtype=jnp.int32))
    layout = [jnp.transpose(piece, (1, 0, 2)).reshape(D, EXPERTS * HID) for piece in stacked]
    return final[:TOKENS], layout[0], layout[1], layout[2]


def reference(layer_input, out_grad, routes, gates, w_gate, w_up, w_down):
    passes, gate_list, up_list, down_list = [], [], [], []
    for section in range(SECTIONS):
        token_grad, grad_gate, grad_up, grad_down = section_math(layer_input[section], out_grad[section], routes[section, :, 0], gates[section], w_gate[section], w_up[section], w_down[section])
        passes.append(token_grad)
        gate_list.append(grad_gate)
        up_list.append(grad_up)
        down_list.append(grad_down)
    passed_grad = jnp.roll(jnp.stack(passes), -1, axis=0)
    return passed_grad, jnp.stack(gate_list), jnp.stack(up_list), jnp.stack(down_list)
```

```python
import functools

import jax
import jax.numpy as jnp
from jax import lax
from jax.experimental import pallas as pl
from jax.experimental.pallas import tpu as pltpu
from jax.sharding import PartitionSpec as P

F32, BF16 = jnp.float32, jnp.bfloat16
OUTER = (((0,), (0,)), ((), ()))
INNER = (((1,), (1,)), ((), ()))


def along_z(i, step, zs, xs):
    return (i // xs + step) % zs * xs + i % xs


def to_mate(i, xs):
    return i ^ 1


def to_other(i, xs):
    x = i % xs
    return i - x + (x + (1 if x % 2 else -1)) % xs


def to_diagonal(i, xs):
    x = i % xs
    return i - x + (x + 2) % xs


def moved(block, place):
    return lax.ppermute(block, "expert", [(i, place(i)) for i in range(lax.axis_size("expert"))])


def after(value, *earlier):
    return lax.optimization_barrier((value,) + earlier)[0]


def activations(gate_pre, up_pre, d_hidden):
    sigmoid_gate = jax.nn.sigmoid(gate_pre)
    silu_gate = gate_pre * sigmoid_gate
    hidden = (silu_gate * up_pre).astype(BF16)
    d_up = (d_hidden * silu_gate).astype(BF16)
    d_gate = (d_hidden * up_pre * sigmoid_gate * (1.0 + gate_pre * (1.0 - sigmoid_gate))).astype(BF16)
    return hidden, d_gate, d_up


def forward_kernel(counts, capacity, *refs):
    pieces, (weights,) = refs[:len(counts)], refs[len(counts):len(counts) + 1]
    flat_x, flat_dy, hidden, d_gate, d_up, sums = refs[len(counts) + 1:]
    step = pl.program_id(0)
    cut = weights.shape[1]
    here = pl.ds(pl.multiple_of(step * cut, cut), cut)
    at = 0
    for piece, count in zip(pieces, counts):
        for j in range(count):
            low = 2 * capacity * j
            flat_x[at:at + capacity, here] = piece[low:low + capacity, here]
            flat_dy[at:at + capacity, here] = piece[low + capacity:low + 2 * capacity, here]
            at += capacity

    @pl.when(step == 0)
    def _():
        sums[...] = jnp.zeros_like(sums)

    x, dy = flat_x[:, here], flat_dy[:, here]
    sums[0] += jnp.dot(x, weights[0], preferred_element_type=F32)
    sums[1] += jnp.dot(x, weights[1], preferred_element_type=F32)
    sums[2] += jnp.dot(dy, weights[2], preferred_element_type=F32)

    @pl.when(step == pl.num_programs(0) - 1)
    def _():
        out = activations(sums[0], sums[1], sums[2])
        hidden[...], d_gate[...], d_up[...] = out


def forward(pieces, weights, capacity):
    counts = [p.shape[0] // (2 * capacity) for p in pieces]
    rows = sum(counts) * capacity
    width, half = weights.shape[1:]
    cut = 512
    flat = jax.ShapeDtypeStruct((rows, width), BF16)
    small = jax.ShapeDtypeStruct((rows, half), BF16)
    return pl.pallas_call(
        functools.partial(forward_kernel, counts, capacity),
        grid=(width // cut,),
        in_specs=[pl.BlockSpec(memory_space=pltpu.VMEM)] * len(pieces)
        + [pl.BlockSpec((3, cut, half), lambda k: (0, k, 0))],
        out_specs=[pl.BlockSpec(memory_space=pltpu.VMEM)] * 5,
        out_shape=[flat, flat, small, small, small],
        scratch_shapes=[pltpu.VMEM((3, rows, half), F32)],
        compiler_params=pltpu.CompilerParams(vmem_limit_bytes=32 * 2**20),
        cost_estimate=pl.CostEstimate(
            flops=6 * rows * width * half, bytes_accessed=30 * 2**20, transcendentals=rows * half
        ),
    )(*pieces, weights)


def chunk_at(term, offset):
    place = (lax.axis_index("dp") + offset) % 4
    return lax.dynamic_index_in_dim(term, place, 0, keepdims=False)


def y_shift(block, step):
    n = lax.axis_size("dp")
    return lax.ppermute(block, "dp", [(i, (i + step) % n) for i in range(n)])


def ring_first(term):
    far = chunk_at(term, 2)
    half = far.shape[0] // 2
    return y_shift(far[:half], 1), y_shift(far[half:], -1)


def ring_second(term, first):
    half = first[0].shape[0]
    up, down = chunk_at(term, 1), chunk_at(term, 3)
    head = (up[:half].astype(F32) + first[0].astype(F32)).astype(BF16)
    tail = (down[half:].astype(F32) + first[1].astype(F32)).astype(BF16)
    return (
        y_shift(jnp.concatenate([head, up[half:]], 0), 1),
        y_shift(jnp.concatenate([down[:half], tail], 0), -1),
    )


def ring_sum(term, second):
    return chunk_at(term, 0).astype(F32) + second[0].astype(F32) + second[1].astype(F32)


def local(layer_input, out_grad, routes, gates, w_gate, w_up, w_down):
    dev_count = lax.axis_size("expert")
    xs, zs = 4, dev_count // 4
    tok_rows, width = layer_input.shape[1:]
    experts = dev_count // 2
    capacity = 2 * tok_rows // experts
    me = lax.axis_index("expert")
    my_z, my_pair = me // xs, me % xs // 2

    tokens = layer_input[0]
    scaled = (gates[0][:, None] * out_grad[0].astype(F32)).astype(BF16)
    target = routes[0, :, 0]
    onehot = (target[:, None] == jnp.arange(experts, dtype=jnp.int32)[None, :]).astype(jnp.int32)
    before = jnp.cumsum(onehot, axis=0) - onehot
    rank = jnp.sum(before * onehot, axis=1)
    step = (target // 2 - my_z) % zs
    side = (target % 2) ^ my_pair
    home_column = (side * zs + target // 2) * capacity + rank
    other_column = lax.ppermute(home_column.astype(F32), "pipe", [(0, 1), (1, 0)])
    both = jnp.concatenate([tokens, scaled], axis=0)
    row_x = (step * 2 + side) * 2 * capacity + rank
    row_of = jnp.concatenate([row_x, row_x + capacity], axis=0)
    block_rows = 4 * capacity
    weights = lax.all_gather(jnp.stack([w_gate[0], w_up[0], w_down[0]], 0), "dp", axis=1, tiled=True)

    def block(s):
        rows = jnp.arange(block_rows, dtype=jnp.int32) + s * block_rows
        pick = (rows[:, None] == row_of[None, :]).astype(BF16)
        return jnp.dot(pick, both, preferred_element_type=F32).astype(BF16)

    blocks = [block(s) for s in range(zs)]
    here = {0: blocks[0]}

    def send(s, *earlier):
        data = after(blocks[s], *earlier) if earlier else blocks[s]
        here[s] = moved(data, lambda i: along_z(i, s, zs, xs))

    def spread(steps, *earlier):
        stacked = [here[s].reshape(2, 2 * capacity, width) for s in steps]
        same = jnp.concatenate([v[0] for v in stacked], 0)
        cross = jnp.concatenate([v[1] for v in stacked], 0)
        if earlier:
            same, cross = lax.optimization_barrier((same, cross) + earlier)[:2]
        return [
            same,
            moved(same, lambda i: to_mate(i, xs)),
            moved(cross, lambda i: to_other(i, xs)),
            moved(cross, lambda i: to_diagonal(i, xs)),
        ]

    def round_of(sends, steps):
        stacked = [here[s].reshape(2, 2 * capacity, width) for s in steps]
        same = jnp.concatenate([v[0] for v in stacked], 0)
        cross = jnp.concatenate([v[1] for v in stacked], 0)
        outs = [same] + [
            moved(same, lambda i: to_mate(i, xs)),
            moved(cross, lambda i: to_other(i, xs)),
            moved(cross, lambda i: to_diagonal(i, xs)),
        ]
        for s in sends:
            outs.append(moved(blocks[s], lambda i, s=s: along_z(i, s, zs, xs)))
        names = [s for r in rounds[len(parts) + 1:] for s in r[0]]
        rest = [blocks[s] for s in names]
        done = lax.optimization_barrier(tuple(outs + rest))
        parts.append(done[:4])
        for s, v in zip(sends, done[4:]):
            here[s] = v
        for s, v in zip(names, done[4 + len(sends):]):
            blocks[s] = v

    rounds = [((1, 7), (0,)), ((2, 6), (1, 7)), ((3, 5), (2, 6)), ((4,), (3, 5)), ((), (4,))]
    parts = []
    for sends, steps in rounds:
        round_of(sends, steps)
    groups = [r[1] for r in rounds]

    pieces = [g[origin] for origin in range(4) for g in parts]
    flat_x, flat_dy, hidden, d_gate, d_up = forward(pieces, weights, capacity)
    gate_full, up_full = weights[0], weights[1]

    def term(rows_in, value):
        t = lax.dot_general(rows_in, value, OUTER, preferred_element_type=F32).astype(BF16)
        return t.reshape(4, t.shape[0] // 4, t.shape[1])

    partial_value = lax.dot_general(d_gate, gate_full, INNER, preferred_element_type=F32)
    partial_value = partial_value + lax.dot_general(d_up, up_full, INNER, preferred_element_type=F32)
    back = partial_value.astype(BF16).reshape(4, zs, capacity, width)
    order = [s for g in groups for s in g]
    cores, zgroups = range(2), [[x + xs * z for z in range(zs)] for x in range(xs)]

    def crossed(block, place):
        route = [(c * dev_count + i, (1 - c) * dev_count + place(i)) for c in cores for i in range(dev_count)]
        return lax.ppermute(block, ("pipe", "expert"), route)

    def by_place(rows_in):
        ring = jnp.concatenate([rows_in[order.index(s)][None] for s in reversed(range(zs))] * 2, 0)
        ring = lax.dynamic_slice_in_dim(ring, (2 * zs - my_z - 1) % zs, zs, 0)
        return lax.all_to_all(ring, "expert", 0, 0, axis_index_groups=zgroups, tiled=True)

    own = crossed(back[0], lambda i: i)
    mate = crossed(back[1], lambda i: to_mate(i, xs))
    other = crossed(back[2], lambda i: to_other(i, xs))
    t_gate = term(flat_x, d_gate)
    r_gate = lax.psum_scatter(t_gate.reshape(width, -1), "dp", scatter_dimension=0, tiled=True)
    t_up = term(flat_x, d_up)
    own, mate, other, last, t_up = lax.optimization_barrier((own, mate, other, back[3], t_up))
    same = by_place((own.astype(F32) + mate.astype(F32)).astype(BF16))
    diag = crossed(last, lambda i: to_diagonal(i, xs))
    s_up = ring_second(t_up, ring_first(t_up))
    t_down = term(flat_dy, hidden)
    same, other, diag, t_down, *s_up = lax.optimization_barrier((same, other, diag, t_down, *s_up))
    cross = by_place((other.astype(F32) + diag.astype(F32)).astype(BF16))
    s_down = ring_second(t_down, ring_first(t_down))
    summed = jnp.concatenate([same, cross], 0).reshape(2 * zs * capacity, width)
    slots = jnp.arange(2 * zs * capacity, dtype=jnp.int32)
    combine = (slots[None, :] == other_column.astype(jnp.int32)[:, None]).astype(BF16)
    passed = jnp.dot(combine, summed, preferred_element_type=F32).astype(BF16)
    return (
        passed[None],
        r_gate.astype(F32)[None],
        ring_sum(t_up, s_up)[None],
        ring_sum(t_down, s_down)[None],
    )


def solution(mesh):
    placed = (
        P("pipe", ("expert", "dp"), None),
        P("pipe", ("expert", "dp"), None),
        P("pipe", ("expert", "dp"), None),
        P("pipe", ("expert", "dp")),
        P("pipe", "dp", "expert"),
        P("pipe", "dp", "expert"),
        P("pipe", "dp", "expert"),
    )
    return jax.shard_map(
        local,
        mesh=mesh,
        in_specs=placed,
        out_specs=(
            P("pipe", ("expert", "dp"), None),
            P("pipe", "dp", "expert"),
            P("pipe", "dp", "expert"),
            P("pipe", "dp", "expert"),
        ),
        check_vma=False,
    )
```

```python
import functools

import jax
import jax.numpy as jnp
from jax import lax
from jax.experimental import pallas as pl
from jax.experimental.pallas import tpu as pltpu
from jax.sharding import PartitionSpec as P

F32, BF16 = jnp.float32, jnp.bfloat16
OUTER = (((0,), (0,)), ((), ()))
INNER = (((1,), (1,)), ((), ()))


def along_z(i, step, zs, xs):
    return (i // xs + step) % zs * xs + i % xs


def to_mate(i, xs):
    return i ^ 1


def to_other(i, xs):
    x = i % xs
    return i - x + (x + (1 if x % 2 else -1)) % xs


def to_diagonal(i, xs):
    x = i % xs
    return i - x + (x + 2) % xs


def moved(block, place):
    return lax.ppermute(block, "expert", [(i, place(i)) for i in range(lax.axis_size("expert"))])


def after(value, *earlier):
    return lax.optimization_barrier((value,) + earlier)[0]


def activations(gate_pre, up_pre, d_hidden):
    sigmoid_gate = jax.nn.sigmoid(gate_pre)
    silu_gate = gate_pre * sigmoid_gate
    hidden = (silu_gate * up_pre).astype(BF16)
    d_up = (d_hidden * silu_gate).astype(BF16)
    d_gate = (d_hidden * up_pre * sigmoid_gate * (1.0 + gate_pre * (1.0 - sigmoid_gate))).astype(BF16)
    return hidden, d_gate, d_up


def expert_kernel(counts, last, capacity, *refs):
    pieces, refs = refs[:len(counts)], refs[len(counts):]
    weights, refs = refs[0], refs[1:]
    if last:
        early, refs = refs[0], refs[1:]
    flat_x, flat_dy, hidden, slopes, *backs = refs[:-4]
    sums, held, arrived, loaded = refs[-4:]
    width, half = flat_x.shape[1], hidden.shape[1]
    halves, cut = 2, 1024
    wide = width // halves
    loads = [
        pltpu.make_async_copy(
            weights.at[:, pl.ds(c * cut, cut), :], held.at[:, pl.ds(c * cut, cut), :], loaded.at[c]
        )
        for c in range(width // cut)
    ]
    for h in range(halves):
        columns = pl.ds(h * wide, wide)
        at = 0
        for piece, count in zip(pieces, counts):
            rows = count * capacity
            for part, flat in enumerate((flat_x, flat_dy)):
                pltpu.make_async_copy(
                    piece.at[pl.ds(part * rows, rows), columns],
                    flat.at[pl.ds(at, rows), columns],
                    arrived.at[part, h],
                ).start()
            at += rows
        for c in range(h * wide // cut, (h + 1) * wide // cut):
            loads[c].start()
    sums[...] = jnp.zeros_like(sums)
    for h in range(halves):
        columns = pl.ds(h * wide, wide)
        for part, flat in enumerate((flat_x, flat_dy)):
            whole = flat.at[:, columns]
            pltpu.make_async_copy(whole, whole, arrived.at[part, h]).wait()

        for c in range(h * wide // cut, (h + 1) * wide // cut):
            loads[c].wait()
            here = pl.ds(c * cut, cut)
            x, dy = flat_x[:, here], flat_dy[:, here]
            sums[0] += jnp.dot(x, held[0, here, :], preferred_element_type=F32)
            sums[1] += jnp.dot(x, held[1, here, :], preferred_element_type=F32)
            sums[2] += jnp.dot(dy, held[2, here, :], preferred_element_type=F32)

    hidden[...], slopes[:, :half], slopes[:, half:] = activations(sums[0], sums[1], sums[2])
    if not last:
        return
    cut = 512

    @pl.loop(0, width // cut)
    def _(k):
        here = pl.ds(pl.multiple_of(k * cut, cut), cut)
        for source, outs in ((slopes, backs[:4]), (early, backs[4:])):
            value = lax.dot_general(source[:, :half], held[0, here, :], INNER, preferred_element_type=F32)
            value += lax.dot_general(source[:, half:], held[1, here, :], INNER, preferred_element_type=F32)
            value = value.astype(BF16)
            rows = source.shape[0] // 4
            for i, back in enumerate(outs):
                back[:, here] = value[i * rows:(i + 1) * rows]


def expert_block(pieces, weights, early, capacity):
    counts = [p.shape[0] // (2 * capacity) for p in pieces]
    rows = sum(counts) * capacity
    width, half = weights.shape[1:]
    last = early is not None
    out_shape = [jax.ShapeDtypeStruct((rows, width), BF16)] * 2
    out_shape += [jax.ShapeDtypeStruct((rows, half), BF16), jax.ShapeDtypeStruct((rows, 2 * half), BF16)]
    if last:
        for count in (rows, early.shape[0]):
            out_shape += [jax.ShapeDtypeStruct((count // 4, width), BF16)] * 4
    in_vmem = pl.BlockSpec(memory_space=pltpu.VMEM)
    return pl.pallas_call(
        functools.partial(expert_kernel, counts, last, capacity),
        in_specs=[pl.BlockSpec(memory_space=pl.ANY)] * (len(pieces) + 1) + [in_vmem] * last,
        out_specs=[in_vmem] * len(out_shape),
        out_shape=out_shape,
        scratch_shapes=[
            pltpu.VMEM((3, rows, half), F32),
            pltpu.VMEM(weights.shape, BF16),
            pltpu.SemaphoreType.DMA((2, 2)),
            pltpu.SemaphoreType.DMA((width // 1024,)),
        ],
        compiler_params=pltpu.CompilerParams(vmem_limit_bytes=40 * 2**20),
        cost_estimate=pl.CostEstimate(
            flops=6 * rows * width * half, bytes_accessed=20 * 2**20, transcendentals=rows * half
        ),
    )(*pieces, weights, *([early] if last else []))


def outer_kernel(cut, rows_early, rows_late, d_early, d_late, out):
    @pl.loop(0, rows_early.shape[1] // cut)
    def _(k):
        here = pl.ds(pl.multiple_of(k * cut, cut), cut)
        value = lax.dot_general(rows_early[:, here], d_early[...], OUTER, preferred_element_type=F32)
        value += lax.dot_general(rows_late[:, here], d_late[...], OUTER, preferred_element_type=F32)
        out[here, :] = value.astype(BF16)


def outer_term(rows_early, rows_late, d_early, d_late):
    in_vmem = pl.BlockSpec(memory_space=pltpu.VMEM)
    return pl.pallas_call(
        functools.partial(outer_kernel, 512),
        in_specs=[in_vmem] * 4,
        out_specs=in_vmem,
        out_shape=jax.ShapeDtypeStruct((rows_early.shape[1], d_early.shape[1]), BF16),
        compiler_params=pltpu.CompilerParams(vmem_limit_bytes=40 * 2**20),
        cost_estimate=pl.CostEstimate(flops=0, bytes_accessed=0, transcendentals=0),
    )(rows_early, rows_late, d_early, d_late)


def local(layer_input, out_grad, routes, gates, w_gate, w_up, w_down):
    dev_count = lax.axis_size("expert")
    xs, zs = 4, dev_count // 4
    tok_rows, width = layer_input.shape[1:]
    experts = dev_count // 2
    capacity = 2 * tok_rows // experts
    me = lax.axis_index("expert")
    my_z, my_pair = me // xs, me % xs // 2

    tokens = layer_input[0]
    scaled = (gates[0][:, None] * out_grad[0].astype(F32)).astype(BF16)
    target = routes[0, :, 0]
    onehot = (target[:, None] == jnp.arange(experts, dtype=jnp.int32)[None, :]).astype(jnp.int32)
    before = jnp.cumsum(onehot, axis=0) - onehot
    rank = jnp.sum(before * onehot, axis=1)
    step = (target // 2 - my_z) % zs
    side = (target % 2) ^ my_pair
    home_column = (step * 2 + side) * capacity + rank
    other_column = lax.ppermute(home_column.astype(F32), "pipe", [(0, 1), (1, 0)])
    both = jnp.concatenate([tokens, scaled], axis=0)
    row_x = (step * 2 + side) * 2 * capacity + rank
    row_of = jnp.concatenate([row_x, row_x + capacity], axis=0)
    block_rows = 4 * capacity
    weights = lax.all_gather(jnp.stack([w_gate[0], w_up[0], w_down[0]], 0), "dp", axis=1, tiled=True)

    def block(s):
        rows = jnp.arange(block_rows, dtype=jnp.int32) + s * block_rows
        pick = (rows[:, None] == row_of[None, :]).astype(BF16)
        return jnp.dot(pick, both, preferred_element_type=F32).astype(BF16)

    blocks = [block(s) for s in range(zs)]
    here = {0: blocks[0]}

    def round_of(sends, steps, *more):
        stacked = [here[s].reshape(2, 2, capacity, width) for s in steps]
        same = jnp.concatenate([v[0, part] for part in range(2) for v in stacked], 0)
        cross = jnp.concatenate([v[1, part] for part in range(2) for v in stacked], 0)
        outs = [same] + [
            moved(same, lambda i: to_mate(i, xs)),
            moved(cross, lambda i: to_other(i, xs)),
            moved(cross, lambda i: to_diagonal(i, xs)),
        ]
        for s in sends:
            outs.append(moved(blocks[s], lambda i, s=s: along_z(i, s, zs, xs)))
        names = [s for r in rounds[len(parts) + 1:] for s in r[0]]
        rest = [blocks[s] for s in names]
        done = lax.optimization_barrier(tuple(outs + rest) + more)
        parts.append(done[:4])
        for s, v in zip(sends, done[4:]):
            here[s] = v
        for s, v in zip(names, done[4 + len(sends):]):
            blocks[s] = v
        return done[len(done) - len(more):]

    rounds = [((1, 7), (0,)), ((2, 6), (1, 7)), ((3, 5), (2, 6)), ((4,), (3, 5)), ((), (4,))]
    parts = []
    for sends, steps in rounds[:3]:
        round_of(sends, steps)

    def block_of(some, early):
        pieces = [g[origin] for origin in range(4) for g in some]
        return expert_block(pieces, weights, early, capacity)

    early = block_of(parts, None)
    early = round_of(*rounds[3], *early)
    early = round_of(*rounds[4], *early)
    late = block_of(parts[3:], early[3])
    rows_x, rows_dy, hidden, slopes = zip(early, late[:4])
    term = outer_term(*rows_x, *slopes)
    half = hidden[0].shape[1]
    r_both = lax.psum_scatter(term, "dp", scatter_dimension=0, tiled=True)
    term = outer_term(*rows_dy, *hidden)
    r_down = lax.all_to_all(term.reshape(4, width // 4, half), "dp", 0, 0, tiled=True)

    def returned(back):
        return [
            moved(back[1], lambda i: to_mate(i, xs)),
            moved(back[2], lambda i: to_other(i, xs)),
            moved(back[3], lambda i: to_diagonal(i, xs)),
        ]

    def summed(back, came, steps):
        same = (back[0].astype(F32) + came[0].astype(F32)).astype(BF16)
        cross = (came[1].astype(F32) + came[2].astype(F32)).astype(BF16)
        for k, s in enumerate(steps):
            cut = slice(k * capacity, (k + 1) * capacity)
            homes[s] = jnp.concatenate([same[cut], cross[cut]], 0)

    def home(s):
        route = [
            (c * dev_count + i, (1 - c) * dev_count + along_z(i, -s, zs, xs))
            for c in range(2) for i in range(dev_count)
        ]
        return lax.ppermute(homes[s], ("pipe", "expert"), route)

    homes = {}
    late_steps = [s for r in rounds[3:] for s in r[1]]
    early_steps = [s for r in rounds[:3] for s in r[1]]
    back_late, back_early = late[4:8], late[8:]
    *came, b0, b1, b2, b3 = lax.optimization_barrier((*returned(back_late), *back_early))
    back_early = [b0, b1, b2, b3]
    summed(back_late, came, late_steps)
    came = returned(back_early)
    far = {s: home(s) for s in late_steps}
    *came, f0, f1, f2, r_down = lax.optimization_barrier((*came, *[far[s] for s in late_steps], r_down))
    summed(back_early, came, early_steps)
    homes = {s: home(s) for s in early_steps} | dict(zip(late_steps, (f0, f1, f2)))
    summed_rows = jnp.concatenate([homes[s] for s in range(zs)], 0)
    slots = jnp.arange(2 * zs * capacity, dtype=jnp.int32)
    combine = (slots[None, :] == other_column.astype(jnp.int32)[:, None]).astype(BF16)
    passed = jnp.dot(combine, summed_rows, preferred_element_type=F32).astype(BF16)
    return (
        passed[None],
        r_both[:, :half].astype(F32)[None],
        r_both[:, half:].astype(F32)[None],
        jnp.sum(r_down.astype(F32), axis=0)[None],
    )


def solution(mesh):
    placed = (
        P("pipe", ("expert", "dp"), None),
        P("pipe", ("expert", "dp"), None),
        P("pipe", ("expert", "dp"), None),
        P("pipe", ("expert", "dp")),
        P("pipe", "dp", "expert"),
        P("pipe", "dp", "expert"),
        P("pipe", "dp", "expert"),
    )
    return jax.shard_map(
        local,
        mesh=mesh,
        in_specs=placed,
        out_specs=(
            P("pipe", ("expert", "dp"), None),
            P("pipe", "dp", "expert"),
            P("pipe", "dp", "expert"),
            P("pipe", "dp", "expert"),
        ),
        check_vma=False,
    )
```

```python
import functools

import jax
import jax.numpy as jnp
from jax import lax
from jax.experimental import pallas as pl
from jax.experimental.pallas import tpu as pltpu
from jax.sharding import PartitionSpec as P

F32, BF16 = jnp.float32, jnp.bfloat16
OUTER = (((0,), (0,)), ((), ()))
INNER = (((1,), (1,)), ((), ()))


def along_z(i, step, zs, xs):
    return (i // xs + step) % zs * xs + i % xs


def to_mate(i, xs):
    return i ^ 1


def to_other(i, xs):
    x = i % xs
    return i - x + (x + (1 if x % 2 else -1)) % xs


def to_diagonal(i, xs):
    x = i % xs
    return i - x + (x + 2) % xs


def moved(block, place):
    return lax.ppermute(block, "expert", [(i, place(i)) for i in range(lax.axis_size("expert"))])


def after(value, *earlier):
    return lax.optimization_barrier((value,) + earlier)[0]


def activations(gate_pre, up_pre, d_hidden):
    sigmoid_gate = jax.nn.sigmoid(gate_pre)
    silu_gate = gate_pre * sigmoid_gate
    hidden = (silu_gate * up_pre).astype(BF16)
    d_up = (d_hidden * silu_gate).astype(BF16)
    d_gate = (d_hidden * up_pre * sigmoid_gate * (1.0 + gate_pre * (1.0 - sigmoid_gate))).astype(BF16)
    return hidden, d_gate, d_up


def expert_kernel(counts, capacity, *refs):
    pieces, refs = refs[:len(counts)], refs[len(counts):]
    weights, out_x, out_dy, hidden, slopes, flat_x, flat_dy, sums, held, arrived, loaded, kept = refs
    width, half = flat_x.shape[1], hidden.shape[1]
    halves, cut = 2, 1024
    wide = width // halves
    loads = [
        pltpu.make_async_copy(
            weights.at[:, pl.ds(c * cut, cut), :], held.at[:, pl.ds(c * cut, cut), :], loaded.at[c]
        )
        for c in range(width // cut)
    ]
    for h in range(halves):
        columns = pl.ds(h * wide, wide)
        at = 0
        for piece, count in zip(pieces, counts):
            rows = count * capacity
            for part, flat in enumerate((flat_x, flat_dy)):
                pltpu.make_async_copy(
                    piece.at[pl.ds(part * rows, rows), columns],
                    flat.at[pl.ds(at, rows), columns],
                    arrived.at[part, h],
                ).start()
            at += rows
        for c in range(h * wide // cut, (h + 1) * wide // cut):
            loads[c].start()
    sums[...] = jnp.zeros_like(sums)
    keeps = []
    for h in range(halves):
        columns = pl.ds(h * wide, wide)
        for part, (flat, out) in enumerate(((flat_x, out_x), (flat_dy, out_dy))):
            whole = flat.at[:, columns]
            pltpu.make_async_copy(whole, whole, arrived.at[part, h]).wait()
            keep = pltpu.make_async_copy(whole, out.at[:, columns], kept.at[part, h])
            keep.start()
            keeps.append(keep)
        for c in range(h * wide // cut, (h + 1) * wide // cut):
            loads[c].wait()
            here = pl.ds(c * cut, cut)
            x, dy = flat_x[:, here], flat_dy[:, here]
            sums[0] += jnp.dot(x, held[0, here, :], preferred_element_type=F32)
            sums[1] += jnp.dot(x, held[1, here, :], preferred_element_type=F32)
            sums[2] += jnp.dot(dy, held[2, here, :], preferred_element_type=F32)

    hidden[...], slopes[:, :half], slopes[:, half:] = activations(sums[0], sums[1], sums[2])
    for keep in keeps:
        keep.wait()


def expert_block(pieces, weights, capacity):
    counts = [p.shape[0] // (2 * capacity) for p in pieces]
    rows = sum(counts) * capacity
    width, half = weights.shape[1:]
    anywhere, whole = pl.BlockSpec(memory_space=pl.ANY), pl.BlockSpec()
    return pl.pallas_call(
        functools.partial(expert_kernel, counts, capacity),
        in_specs=[anywhere] * (len(pieces) + 1),
        out_specs=[anywhere, anywhere, whole, whole],
        out_shape=[
            jax.ShapeDtypeStruct((rows, width), BF16),
            jax.ShapeDtypeStruct((rows, width), BF16),
            jax.ShapeDtypeStruct((rows, half), BF16),
            jax.ShapeDtypeStruct((rows, 2 * half), BF16),
        ],
        scratch_shapes=[
            pltpu.VMEM((rows, width), BF16),
            pltpu.VMEM((rows, width), BF16),
            pltpu.VMEM((3, rows, half), F32),
            pltpu.VMEM(weights.shape, BF16),
            pltpu.SemaphoreType.DMA((2, 2)),
            pltpu.SemaphoreType.DMA((width // 1024,)),
            pltpu.SemaphoreType.DMA((2, 2)),
        ],
        compiler_params=pltpu.CompilerParams(vmem_limit_bytes=40 * 2**20),
        cost_estimate=pl.CostEstimate(
            flops=6 * rows * width * half, bytes_accessed=20 * 2**20, transcendentals=rows * half
        ),
    )(*pieces, weights)


def back_kernel(slopes, weights, *backs):
    half = weights.shape[2]
    value = lax.dot_general(slopes[:, :half], weights[0], INNER, preferred_element_type=F32)
    value += lax.dot_general(slopes[:, half:], weights[1], INNER, preferred_element_type=F32)
    value = value.astype(BF16)
    rows = slopes.shape[0] // 4
    for i, back in enumerate(backs):
        back[...] = value[i * rows:(i + 1) * rows]


def back_block(slopes, weights):
    rows, (width, half), cut = slopes.shape[0], weights.shape[1:], 1024
    return pl.pallas_call(
        back_kernel,
        grid=(width // cut,),
        in_specs=[
            pl.BlockSpec((rows, 2 * half), lambda k: (0, 0)),
            pl.BlockSpec((2, cut, half), lambda k: (0, k, 0)),
        ],
        out_specs=[pl.BlockSpec((rows // 4, cut), lambda k: (0, k))] * 4,
        out_shape=[jax.ShapeDtypeStruct((rows // 4, width), BF16)] * 4,
        compiler_params=pltpu.CompilerParams(vmem_limit_bytes=32 * 2**20),
        cost_estimate=pl.CostEstimate(
            flops=4 * rows * width * half, bytes_accessed=9 * 2**20, transcendentals=0
        ),
    )(slopes, weights)


def outer_kernel(x_early, x_late, dy_early, dy_late, slopes_early, slopes_late, hidden_early, hidden_late, out):
    def product(rows, values):
        return lax.dot_general(rows[...], values[...], OUTER, preferred_element_type=F32)

    both = slopes_early.shape[1]
    out[:, :both] = (product(x_early, slopes_early) + product(x_late, slopes_late)).astype(BF16)
    out[:, both:] = (product(dy_early, hidden_early) + product(dy_late, hidden_late)).astype(BF16)


def outer_terms(rows_x, rows_dy, slopes, hidden):
    width, cut = rows_x[0].shape[1], 512
    columns = slopes[0].shape[1] + hidden[0].shape[1]
    return pl.pallas_call(
        outer_kernel,
        grid=(width // cut,),
        in_specs=[pl.BlockSpec((v.shape[0], cut), lambda k: (0, k)) for v in (*rows_x, *rows_dy)]
        + [pl.BlockSpec(v.shape, lambda k: (0, 0)) for v in (*slopes, *hidden)],
        out_specs=pl.BlockSpec((cut, columns), lambda k: (k, 0)),
        out_shape=jax.ShapeDtypeStruct((width, columns), BF16),
        compiler_params=pltpu.CompilerParams(vmem_limit_bytes=32 * 2**20),
        cost_estimate=pl.CostEstimate(flops=0, bytes_accessed=0, transcendentals=0),
    )(*rows_x, *rows_dy, *slopes, *hidden)


def local(layer_input, out_grad, routes, gates, w_gate, w_up, w_down):
    dev_count = lax.axis_size("expert")
    xs, zs = 4, dev_count // 4
    tok_rows, width = layer_input.shape[1:]
    experts = dev_count // 2
    capacity = 2 * tok_rows // experts
    me = lax.axis_index("expert")
    my_z, my_pair = me // xs, me % xs // 2

    tokens = layer_input[0]
    scaled = (gates[0][:, None] * out_grad[0].astype(F32)).astype(BF16)
    target = routes[0, :, 0]
    onehot = (target[:, None] == jnp.arange(experts, dtype=jnp.int32)[None, :]).astype(jnp.int32)
    before = jnp.cumsum(onehot, axis=0) - onehot
    rank = jnp.sum(before * onehot, axis=1)
    step = (target // 2 - my_z) % zs
    side = (target % 2) ^ my_pair
    home_column = (step * 2 + side) * capacity + rank
    other_column = lax.ppermute(home_column.astype(F32), "pipe", [(0, 1), (1, 0)])
    both = jnp.concatenate([tokens, scaled], axis=0)
    row_x = (step * 2 + side) * 2 * capacity + rank
    row_of = jnp.concatenate([row_x, row_x + capacity], axis=0)
    block_rows = 4 * capacity

    def block(s):
        rows = jnp.arange(block_rows, dtype=jnp.int32) + s * block_rows
        pick = (rows[:, None] == row_of[None, :]).astype(BF16)
        return jnp.dot(pick, both, preferred_element_type=F32).astype(BF16)

    blocks = [block(s) for s in range(zs)]
    here = {0: blocks[0]}
    shards = lax.optimization_barrier((w_gate, w_up, w_down, blocks[4]))[:3]
    weights = lax.all_gather(jnp.concatenate(shards, 0), "dp", axis=1, tiled=True)

    def round_of(sends, steps, *more):
        stacked = [here[s].reshape(2, 2, capacity, width) for s in steps]
        same = jnp.concatenate([v[0, part] for part in range(2) for v in stacked], 0)
        cross = jnp.concatenate([v[1, part] for part in range(2) for v in stacked], 0)
        outs = [same] + [
            moved(same, lambda i: to_mate(i, xs)),
            moved(cross, lambda i: to_other(i, xs)),
            moved(cross, lambda i: to_diagonal(i, xs)),
        ]
        for s in sends:
            outs.append(moved(blocks[s], lambda i, s=s: along_z(i, s, zs, xs)))
        names = [s for r in rounds[len(parts) + 1:] for s in r[0]]
        rest = [blocks[s] for s in names]
        done = lax.optimization_barrier(tuple(outs + rest) + more)
        parts.append(done[:4])
        for s, v in zip(sends, done[4:]):
            here[s] = v
        for s, v in zip(names, done[4 + len(sends):]):
            blocks[s] = v
        return done[len(done) - len(more):]

    rounds = [((1, 7), (0,)), ((2, 6), (1, 7)), ((3, 5), (2, 6)), ((4,), (3, 5)), ((), (4,))]
    parts = []
    for sends, steps in rounds[:3]:
        round_of(sends, steps)

    def block_of(some):
        pieces = [g[origin] for origin in range(4) for g in some]
        return expert_block(pieces, weights, capacity)

    early = block_of(parts)
    early = round_of(*rounds[3], *early)
    early = tuple(early) + tuple(back_block(early[3], weights))
    early = round_of(*rounds[4], *early)

    def returned(back):
        return [
            moved(back[1], lambda i: to_mate(i, xs)),
            moved(back[2], lambda i: to_other(i, xs)),
            moved(back[3], lambda i: to_diagonal(i, xs)),
        ]

    def summed(back, came, steps):
        same = (back[0].astype(F32) + came[0].astype(F32)).astype(BF16)
        cross = (came[1].astype(F32) + came[2].astype(F32)).astype(BF16)
        for k, s in enumerate(steps):
            cut = slice(k * capacity, (k + 1) * capacity)
            homes[s] = jnp.concatenate([same[cut], cross[cut]], 0)

    def home(s):
        route = [
            (c * dev_count + i, (1 - c) * dev_count + along_z(i, -s, zs, xs))
            for c in range(2) for i in range(dev_count)
        ]
        return lax.ppermute(homes[s], ("pipe", "expert"), route)

    homes = {}
    late_steps = [s for r in rounds[3:] for s in r[1]]
    early_steps = [s for r in rounds[:3] for s in r[1]]
    late = block_of(parts[3:])
    hidden_late, *back_early = lax.optimization_barrier((late[2], *early[4:]))
    came = returned(back_early)
    rows_x, rows_dy, hidden, slopes = zip(early[:4], late)
    half = hidden[0].shape[1]
    terms = outer_terms(rows_x, rows_dy, slopes, (hidden[0], hidden_late))
    grads = lax.psum_scatter(terms, "dp", scatter_dimension=0, tiled=True)
    back_late = back_block(after(late[3], terms), weights)
    *came, b0, b1, b2, b3 = lax.optimization_barrier((*came, *back_late))
    summed(early[4:], came, early_steps)
    back_late = [b0, b1, b2, b3]
    came = returned(back_late)
    near = {s: home(s) for s in (2, 6)}
    came = list(lax.optimization_barrier((*came, near[2], near[6], *[homes[s] for s in (0, 1, 7)])))
    near = dict(zip((2, 6), came[3:5]))
    homes.update(zip((0, 1, 7), came[5:8]))
    summed(back_late, came[:3], late_steps)
    homes = {s: home(s) for s in (3, 5, 4, 1, 7, 0)} | near
    summed_rows = jnp.concatenate([homes[s] for s in range(zs)], 0)
    slots = jnp.arange(2 * zs * capacity, dtype=jnp.int32)
    combine = (slots[None, :] == other_column.astype(jnp.int32)[:, None]).astype(BF16)
    passed = jnp.dot(combine, summed_rows, preferred_element_type=F32).astype(BF16)
    return (
        passed[None],
        grads[:, :half].astype(F32)[None],
        grads[:, half:2 * half].astype(F32)[None],
        grads[:, 2 * half:].astype(F32)[None],
    )


def solution(mesh):
    placed = (
        P("pipe", ("expert", "dp"), None),
        P("pipe", ("expert", "dp"), None),
        P("pipe", ("expert", "dp"), None),
        P("pipe", ("expert", "dp")),
        P("pipe", "dp", "expert"),
        P("pipe", "dp", "expert"),
        P("pipe", "dp", "expert"),
    )
    return jax.shard_map(
        local,
        mesh=mesh,
        in_specs=placed,
        out_specs=(
            P("pipe", ("expert", "dp"), None),
            P("pipe", "dp", "expert"),
            P("pipe", "dp", "expert"),
            P("pipe", "dp", "expert"),
        ),
        check_vma=False,
    )
```

```python
import functools

import jax
import jax.numpy as jnp
from jax import lax
from jax.experimental import pallas as pl
from jax.experimental.pallas import tpu as pltpu
from jax.sharding import PartitionSpec as P

F32, BF16 = jnp.float32, jnp.bfloat16
OUTER = (((0,), (0,)), ((), ()))
INNER = (((1,), (1,)), ((), ()))
VMEM_BYTES = 56 * 2**20


def along_z(i, step, zs, xs):
    return (i // xs + step) % zs * xs + i % xs


def to_mate(i, xs):
    return i ^ 1


def to_other(i, xs):
    x = i % xs
    return i - x + (x + (1 if x % 2 else -1)) % xs


def to_diagonal(i, xs):
    x = i % xs
    return i - x + (x + 2) % xs


def moved(block, place):
    return lax.ppermute(block, "expert", [(i, place(i)) for i in range(lax.axis_size("expert"))])


def after(value, *earlier):
    return lax.optimization_barrier((value,) + earlier)[0]


def activations(gate_pre, up_pre, d_hidden):
    sigmoid_gate = jax.nn.sigmoid(gate_pre)
    silu_gate = gate_pre * sigmoid_gate
    hidden = (silu_gate * up_pre).astype(BF16)
    d_up = (d_hidden * silu_gate).astype(BF16)
    d_gate = (d_hidden * up_pre * sigmoid_gate * (1.0 + gate_pre * (1.0 - sigmoid_gate))).astype(BF16)
    return hidden, d_gate, d_up


def expert_kernel(counts, capacity, *refs):
    pieces, refs = refs[:len(counts)], refs[len(counts):]
    weights, out_x, out_dy, hidden, slopes, flat_x, flat_dy, sums, held, arrived, loaded, kept = refs
    width, half = flat_x.shape[1], hidden.shape[1]
    halves, cut = 2, 1024
    wide = width // halves
    loads = [
        pltpu.make_async_copy(
            weights.at[:, pl.ds(c * cut, cut), :], held.at[:, pl.ds(c * cut, cut), :], loaded.at[c]
        )
        for c in range(width // cut)
    ]
    for h in range(halves):
        columns = pl.ds(h * wide, wide)
        at = 0
        for piece, count in zip(pieces, counts):
            rows = count * capacity
            for part, flat in enumerate((flat_x, flat_dy)):
                pltpu.make_async_copy(
                    piece.at[pl.ds(part * rows, rows), columns],
                    flat.at[pl.ds(at, rows), columns],
                    arrived.at[part, h],
                ).start()
            at += rows
        for c in range(h * wide // cut, (h + 1) * wide // cut):
            loads[c].start()
    sums[...] = jnp.zeros_like(sums)
    keeps = []
    for h in range(halves):
        columns = pl.ds(h * wide, wide)
        for part, (flat, out) in enumerate(((flat_x, out_x), (flat_dy, out_dy))):
            whole = flat.at[:, columns]
            pltpu.make_async_copy(whole, whole, arrived.at[part, h]).wait()
            keep = pltpu.make_async_copy(whole, out.at[:, columns], kept.at[part, h])
            keep.start()
            keeps.append(keep)
        for c in range(h * wide // cut, (h + 1) * wide // cut):
            loads[c].wait()
            here = pl.ds(c * cut, cut)
            x, dy = flat_x[:, here], flat_dy[:, here]
            sums[0] += jnp.dot(x, held[0, here, :], preferred_element_type=F32)
            sums[1] += jnp.dot(x, held[1, here, :], preferred_element_type=F32)
            sums[2] += jnp.dot(dy, held[2, here, :], preferred_element_type=F32)

    hidden[...], slopes[:, :half], slopes[:, half:] = activations(sums[0], sums[1], sums[2])
    for keep in keeps:
        keep.wait()


def expert_block(pieces, weights, capacity):
    counts = [p.shape[0] // (2 * capacity) for p in pieces]
    rows = sum(counts) * capacity
    width, half = weights.shape[1:]
    anywhere, whole = pl.BlockSpec(memory_space=pl.ANY), pl.BlockSpec()
    return pl.pallas_call(
        functools.partial(expert_kernel, counts, capacity),
        in_specs=[anywhere] * (len(pieces) + 1),
        out_specs=[anywhere, anywhere, whole, whole],
        out_shape=[
            jax.ShapeDtypeStruct((rows, width), BF16),
            jax.ShapeDtypeStruct((rows, width), BF16),
            jax.ShapeDtypeStruct((rows, half), BF16),
            jax.ShapeDtypeStruct((rows, 2 * half), BF16),
        ],
        scratch_shapes=[
            pltpu.VMEM((rows, width), BF16),
            pltpu.VMEM((rows, width), BF16),
            pltpu.VMEM((3, rows, half), F32),
            pltpu.VMEM(weights.shape, BF16),
            pltpu.SemaphoreType.DMA((2, 2)),
            pltpu.SemaphoreType.DMA((width // 1024,)),
            pltpu.SemaphoreType.DMA((2, 2)),
        ],
        compiler_params=pltpu.CompilerParams(vmem_limit_bytes=VMEM_BYTES),
        cost_estimate=pl.CostEstimate(
            flops=6 * rows * width * half, bytes_accessed=20 * 2**20, transcendentals=rows * half
        ),
    )(*pieces, weights)


def back_kernel(slopes, weights, *backs):
    half = weights.shape[2]
    value = lax.dot_general(slopes[:, :half], weights[0], INNER, preferred_element_type=F32)
    value += lax.dot_general(slopes[:, half:], weights[1], INNER, preferred_element_type=F32)
    value = value.astype(BF16)
    rows = slopes.shape[0] // 4
    for i, back in enumerate(backs):
        back[...] = value[i * rows:(i + 1) * rows]


def back_block(slopes, weights):
    rows, (width, half), cut = slopes.shape[0], weights.shape[1:], 1024
    return pl.pallas_call(
        back_kernel,
        grid=(width // cut,),
        in_specs=[
            pl.BlockSpec((rows, 2 * half), lambda k: (0, 0)),
            pl.BlockSpec((2, cut, half), lambda k: (0, k, 0)),
        ],
        out_specs=[pl.BlockSpec((rows // 4, cut), lambda k: (0, k))] * 4,
        out_shape=[jax.ShapeDtypeStruct((rows // 4, width), BF16)] * 4,
        compiler_params=pltpu.CompilerParams(vmem_limit_bytes=VMEM_BYTES),
        cost_estimate=pl.CostEstimate(
            flops=4 * rows * width * half, bytes_accessed=9 * 2**20, transcendentals=0
        ),
    )(slopes, weights)


def outer_kernel(x_early, x_late, dy_early, dy_late, slopes_early, slopes_late, hidden_early, hidden_late, out):
    def joined(early, late):
        return jnp.concatenate([early[...], late[...]], 0)

    def product(rows, values):
        return lax.dot_general(rows, values, OUTER, preferred_element_type=F32).astype(BF16)

    both = slopes_early.shape[1]
    out[:, :both] = product(joined(x_early, x_late), joined(slopes_early, slopes_late))
    out[:, both:] = product(joined(dy_early, dy_late), joined(hidden_early, hidden_late))


def outer_terms(rows_x, rows_dy, slopes, hidden):
    width, cut = rows_x[0].shape[1], 512
    columns = slopes[0].shape[1] + hidden[0].shape[1]
    return pl.pallas_call(
        outer_kernel,
        grid=(width // cut,),
        in_specs=[pl.BlockSpec((v.shape[0], cut), lambda k: (0, k)) for v in (*rows_x, *rows_dy)]
        + [pl.BlockSpec(v.shape, lambda k: (0, 0)) for v in (*slopes, *hidden)],
        out_specs=pl.BlockSpec((cut, columns), lambda k: (k, 0)),
        out_shape=jax.ShapeDtypeStruct((width, columns), BF16),
        compiler_params=pltpu.CompilerParams(vmem_limit_bytes=VMEM_BYTES),
        cost_estimate=pl.CostEstimate(flops=0, bytes_accessed=0, transcendentals=0),
    )(*rows_x, *rows_dy, *slopes, *hidden)


def local(layer_input, out_grad, routes, gates, w_gate, w_up, w_down):
    dev_count = lax.axis_size("expert")
    xs, zs = 4, dev_count // 4
    tok_rows, width = layer_input.shape[1:]
    experts = dev_count // 2
    capacity = 2 * tok_rows // experts
    me = lax.axis_index("expert")
    my_z, my_pair = me // xs, me % xs // 2

    tokens = layer_input[0]
    scaled = (gates[0][:, None] * out_grad[0].astype(F32)).astype(BF16)
    target = routes[0, :, 0]
    onehot = (target[:, None] == jnp.arange(experts, dtype=jnp.int32)[None, :]).astype(jnp.int32)
    before = jnp.cumsum(onehot, axis=0) - onehot
    rank = jnp.sum(before * onehot, axis=1)
    step = (target // 2 - my_z) % zs
    side = (target % 2) ^ my_pair
    home_column = (step * 2 + side) * capacity + rank
    other_column = lax.ppermute(home_column.astype(F32), "pipe", [(0, 1), (1, 0)])
    both = jnp.concatenate([tokens, scaled], axis=0)
    row_x = (step * 2 + side) * 2 * capacity + rank
    row_of = jnp.concatenate([row_x, row_x + capacity], axis=0)
    block_rows = 4 * capacity

    def block(s):
        rows = jnp.arange(block_rows, dtype=jnp.int32) + s * block_rows
        pick = (rows[:, None] == row_of[None, :]).astype(BF16)
        return jnp.dot(pick, both, preferred_element_type=F32).astype(BF16)

    blocks = [block(s) for s in range(zs)]
    here = {0: blocks[0]}
    shards = lax.optimization_barrier((w_gate, w_up, w_down, blocks[4]))[:3]
    weights = lax.all_gather(jnp.concatenate(shards, 0), "dp", axis=1, tiled=True)

    def round_of(sends, steps, *more):
        outs = []
        if steps:
            stacked = [here[s].reshape(2, 2, capacity, width) for s in steps]
            same = jnp.concatenate([v[0, part] for part in range(2) for v in stacked], 0)
            cross = jnp.concatenate([v[1, part] for part in range(2) for v in stacked], 0)
            outs = [same] + [
                moved(same, lambda i: to_mate(i, xs)),
                moved(cross, lambda i: to_other(i, xs)),
                moved(cross, lambda i: to_diagonal(i, xs)),
            ]
        spread = len(outs)
        for s in sends:
            outs.append(moved(blocks[s], lambda i, s=s: along_z(i, s, zs, xs)))
        names = [s for s in (0, 2, 6, 3, 5, 4) if s not in here]
        rest = [blocks[s] for s in names if s not in sends]
        done = lax.optimization_barrier(tuple(outs + rest) + more)
        if steps:
            parts.append(done[:spread])
        for s, v in zip(sends, done[spread:]):
            here[s] = v
        for s, v in zip([s for s in names if s not in sends], done[spread + len(sends):]):
            blocks[s] = v
        return done[len(done) - len(more):]

    rounds = [((1, 7), ()), ((2, 6), (1, 7)), ((3, 5), (2, 6, 0)), ((4,), (3, 5)), ((), (4,))]
    parts = []
    for sends, steps in rounds[:3]:
        round_of(sends, steps)

    def block_of(some):
        pieces = [g[origin] for origin in range(4) for g in some]
        return expert_block(pieces, weights, capacity)

    early = block_of(parts)
    early = round_of(*rounds[3], *early)
    early = tuple(early) + tuple(back_block(early[3], weights))
    early = round_of(*rounds[4], *early)

    def returned(back):
        return [
            moved(back[1], lambda i: to_mate(i, xs)),
            moved(back[2], lambda i: to_other(i, xs)),
            moved(back[3], lambda i: to_diagonal(i, xs)),
        ]

    def summed(back, came, steps):
        same = (back[0].astype(F32) + came[0].astype(F32)).astype(BF16)
        cross = (came[1].astype(F32) + came[2].astype(F32)).astype(BF16)
        for k, s in enumerate(steps):
            cut = slice(k * capacity, (k + 1) * capacity)
            homes[s] = jnp.concatenate([same[cut], cross[cut]], 0)

    def home(s):
        route = [
            (c * dev_count + i, (1 - c) * dev_count + along_z(i, -s, zs, xs))
            for c in range(2) for i in range(dev_count)
        ]
        return lax.ppermute(homes[s], ("pipe", "expert"), route)

    homes = {}
    late_steps = [s for r in rounds[3:] for s in r[1]]
    early_steps = [s for r in rounds[:3] for s in r[1]]
    late = block_of(parts[2:])
    hidden_late, *back_early = lax.optimization_barrier((late[2], *early[4:]))
    came = returned(back_early)
    rows_x, rows_dy, hidden, slopes = zip(early[:4], late)
    half = hidden[0].shape[1]
    terms = outer_terms(rows_x, rows_dy, slopes, (hidden[0], hidden_late))
    grads = lax.psum_scatter(terms, "dp", scatter_dimension=0, tiled=True)
    back_late = back_block(after(late[3], terms), weights)
    *came, b0, b1, b2, b3 = lax.optimization_barrier((*came, *back_late))
    summed(early[4:], came, early_steps)
    back_late = [b0, b1, b2, b3]
    came = returned(back_late)
    near = {s: home(s) for s in (2, 6)}
    came = list(lax.optimization_barrier((*came, near[2], near[6], *[homes[s] for s in (0, 1, 7)])))
    near = dict(zip((2, 6), came[3:5]))
    homes.update(zip((0, 1, 7), came[5:8]))
    summed(back_late, came[:3], late_steps)
    homes = {s: home(s) for s in (3, 5, 4, 1, 7, 0)} | near
    summed_rows = jnp.concatenate([homes[s] for s in range(zs)], 0)
    slots = jnp.arange(2 * zs * capacity, dtype=jnp.int32)
    combine = (slots[None, :] == other_column.astype(jnp.int32)[:, None]).astype(BF16)
    passed = jnp.dot(combine, summed_rows, preferred_element_type=F32).astype(BF16)
    passed, grads = lax.optimization_barrier((passed, grads))
    return (
        passed[None],
        grads[:, :half].astype(F32)[None],
        grads[:, half:2 * half].astype(F32)[None],
        grads[:, 2 * half:].astype(F32)[None],
    )


def solution(mesh):
    placed = (
        P("pipe", ("expert", "dp"), None),
        P("pipe", ("expert", "dp"), None),
        P("pipe", ("expert", "dp"), None),
        P("pipe", ("expert", "dp")),
        P("pipe", "dp", "expert"),
        P("pipe", "dp", "expert"),
        P("pipe", "dp", "expert"),
    )
    return jax.shard_map(
        local,
        mesh=mesh,
        in_specs=placed,
        out_specs=(
            P("pipe", ("expert", "dp"), None),
            P("pipe", "dp", "expert"),
            P("pipe", "dp", "expert"),
            P("pipe", "dp", "expert"),
        ),
        check_vma=False,
    )
```

```python
import functools

import jax
import jax.numpy as jnp
from jax import lax
from jax.experimental import pallas as pl
from jax.experimental.pallas import tpu as pltpu
from jax.sharding import PartitionSpec as P

F32, BF16 = jnp.float32, jnp.bfloat16
OUTER = (((0,), (0,)), ((), ()))
INNER = (((1,), (1,)), ((), ()))
VMEM_BYTES = 56 * 2**20


def along_z(i, step, zs, xs):
    return (i // xs + step) % zs * xs + i % xs


def to_mate(i, xs):
    return i ^ 1


def to_other(i, xs):
    x = i % xs
    return i - x + (x + (1 if x % 2 else -1)) % xs


def to_diagonal(i, xs):
    x = i % xs
    return i - x + (x + 2) % xs


def moved(block, place):
    return lax.ppermute(block, "expert", [(i, place(i)) for i in range(lax.axis_size("expert"))])


def after(value, *earlier):
    return lax.optimization_barrier((value,) + earlier)[0]


def activations(gate_pre, up_pre, d_hidden):
    sigmoid_gate = jax.nn.sigmoid(gate_pre)
    silu_gate = gate_pre * sigmoid_gate
    hidden = (silu_gate * up_pre).astype(BF16)
    d_up = (d_hidden * silu_gate).astype(BF16)
    d_gate = (d_hidden * up_pre * sigmoid_gate * (1.0 + gate_pre * (1.0 - sigmoid_gate))).astype(BF16)
    return hidden, d_gate, d_up


def expert_kernel(counts, capacity, *refs):
    pieces, refs = refs[:len(counts)], refs[len(counts):]
    weights, out_x, out_dy, hidden, slopes, flat_x, flat_dy, sums, held, arrived, loaded, kept = refs
    width, half = flat_x.shape[1], hidden.shape[1]
    halves, cut = 2, 1024
    wide = width // halves
    loads = [
        pltpu.make_async_copy(
            weights.at[pl.ds(c * cut, cut), :], held.at[pl.ds(c * cut, cut), :], loaded.at[c]
        )
        for c in range(width // cut)
    ]
    for h in range(halves):
        columns = pl.ds(h * wide, wide)
        at = 0
        for piece, count in zip(pieces, counts):
            rows = count * capacity
            for part, flat in enumerate((flat_x, flat_dy)):
                pltpu.make_async_copy(
                    piece.at[pl.ds(part * rows, rows), columns],
                    flat.at[pl.ds(at, rows), columns],
                    arrived.at[part, h],
                ).start()
            at += rows
        for c in range(h * wide // cut, (h + 1) * wide // cut):
            loads[c].start()
    sums[...] = jnp.zeros_like(sums)
    keeps = []
    for h in range(halves):
        columns = pl.ds(h * wide, wide)
        for part, (flat, out) in enumerate(((flat_x, out_x), (flat_dy, out_dy))):
            whole = flat.at[:, columns]
            pltpu.make_async_copy(whole, whole, arrived.at[part, h]).wait()
            keep = pltpu.make_async_copy(whole, out.at[:, columns], kept.at[part, h])
            keep.start()
            keeps.append(keep)
        for c in range(h * wide // cut, (h + 1) * wide // cut):
            loads[c].wait()
            here = pl.ds(c * cut, cut)
            x, dy = flat_x[:, here], flat_dy[:, here]
            sums[:, :2 * half] += jnp.dot(x, held[here, :2 * half], preferred_element_type=F32)
            sums[:, 2 * half:] += jnp.dot(dy, held[here, 2 * half:], preferred_element_type=F32)

    hidden[...], slopes[:, :half], slopes[:, half:] = activations(
        sums[:, :half], sums[:, half:2 * half], sums[:, 2 * half:]
    )
    for keep in keeps:
        keep.wait()


def expert_block(pieces, weights, capacity):
    counts = [p.shape[0] // (2 * capacity) for p in pieces]
    rows = sum(counts) * capacity
    width, half = weights.shape[0], weights.shape[1] // 3
    anywhere, whole = pl.BlockSpec(memory_space=pl.ANY), pl.BlockSpec()
    return pl.pallas_call(
        functools.partial(expert_kernel, counts, capacity),
        in_specs=[anywhere] * (len(pieces) + 1),
        out_specs=[anywhere, anywhere, whole, whole],
        out_shape=[
            jax.ShapeDtypeStruct((rows, width), BF16),
            jax.ShapeDtypeStruct((rows, width), BF16),
            jax.ShapeDtypeStruct((rows, half), BF16),
            jax.ShapeDtypeStruct((rows, 2 * half), BF16),
        ],
        scratch_shapes=[
            pltpu.VMEM((rows, width), BF16),
            pltpu.VMEM((rows, width), BF16),
            pltpu.VMEM((rows, 3 * half), F32),
            pltpu.VMEM(weights.shape, BF16),
            pltpu.SemaphoreType.DMA((2, 2)),
            pltpu.SemaphoreType.DMA((width // 1024,)),
            pltpu.SemaphoreType.DMA((2, 2)),
        ],
        compiler_params=pltpu.CompilerParams(vmem_limit_bytes=VMEM_BYTES),
        cost_estimate=pl.CostEstimate(
            flops=6 * rows * width * half, bytes_accessed=20 * 2**20, transcendentals=rows * half
        ),
    )(*pieces, weights)


def back_kernel(slopes, weights, *backs):
    value = lax.dot_general(slopes[...], weights[...], INNER, preferred_element_type=F32).astype(BF16)
    rows = slopes.shape[0] // 4
    for i, back in enumerate(backs):
        back[...] = value[i * rows:(i + 1) * rows]


def back_block(slopes, weights):
    rows, both = slopes.shape
    width, cut = weights.shape[0], 1024
    return pl.pallas_call(
        back_kernel,
        grid=(width // cut,),
        in_specs=[
            pl.BlockSpec((rows, both), lambda k: (0, 0)),
            pl.BlockSpec((cut, both), lambda k: (k, 0)),
        ],
        out_specs=[pl.BlockSpec((rows // 4, cut), lambda k: (0, k))] * 4,
        out_shape=[jax.ShapeDtypeStruct((rows // 4, width), BF16)] * 4,
        compiler_params=pltpu.CompilerParams(vmem_limit_bytes=VMEM_BYTES),
        cost_estimate=pl.CostEstimate(
            flops=2 * rows * width * both, bytes_accessed=9 * 2**20, transcendentals=0
        ),
    )(slopes, weights)


def outer_kernel(x_early, x_late, dy_early, dy_late, slopes_early, slopes_late, hidden_early, hidden_late, out):
    def joined(early, late):
        return jnp.concatenate([early[...], late[...]], 0)

    def product(rows, values):
        return lax.dot_general(rows, values, OUTER, preferred_element_type=F32).astype(BF16)

    both = slopes_early.shape[1]
    out[:, :both] = product(joined(x_early, x_late), joined(slopes_early, slopes_late))
    out[:, both:] = product(joined(dy_early, dy_late), joined(hidden_early, hidden_late))


def outer_terms(rows_x, rows_dy, slopes, hidden):
    width, cut = rows_x[0].shape[1], 512
    columns = slopes[0].shape[1] + hidden[0].shape[1]
    return pl.pallas_call(
        outer_kernel,
        grid=(width // cut,),
        in_specs=[pl.BlockSpec((v.shape[0], cut), lambda k: (0, k)) for v in (*rows_x, *rows_dy)]
        + [pl.BlockSpec(v.shape, lambda k: (0, 0)) for v in (*slopes, *hidden)],
        out_specs=pl.BlockSpec((cut, columns), lambda k: (k, 0)),
        out_shape=jax.ShapeDtypeStruct((width, columns), BF16),
        compiler_params=pltpu.CompilerParams(vmem_limit_bytes=VMEM_BYTES),
        cost_estimate=pl.CostEstimate(flops=0, bytes_accessed=0, transcendentals=0),
    )(*rows_x, *rows_dy, *slopes, *hidden)


def local(layer_input, out_grad, routes, gates, w_gate, w_up, w_down):
    dev_count = lax.axis_size("expert")
    xs, zs = 4, dev_count // 4
    tok_rows, width = layer_input.shape[1:]
    experts = dev_count // 2
    capacity = 2 * tok_rows // experts
    me = lax.axis_index("expert")
    my_z, my_pair = me // xs, me % xs // 2

    tokens = layer_input[0]
    scaled = (gates[0][:, None] * out_grad[0].astype(F32)).astype(BF16)
    target = routes[0, :, 0]
    onehot = (target[:, None] == jnp.arange(experts, dtype=jnp.int32)[None, :]).astype(jnp.int32)
    before = jnp.cumsum(onehot, axis=0) - onehot
    rank = jnp.sum(before * onehot, axis=1)
    step = (target // 2 - my_z) % zs
    side = (target % 2) ^ my_pair
    home_column = (step * 2 + side) * capacity + rank
    other_column = lax.ppermute(home_column.astype(F32), "pipe", [(0, 1), (1, 0)])
    both = jnp.concatenate([tokens, scaled], axis=0)
    row_x = (step * 2 + side) * 2 * capacity + rank
    row_of = jnp.concatenate([row_x, row_x + capacity], axis=0)
    block_rows = 4 * capacity

    def block(s):
        rows = jnp.arange(block_rows, dtype=jnp.int32) + s * block_rows
        pick = (rows[:, None] == row_of[None, :]).astype(BF16)
        return jnp.dot(pick, both, preferred_element_type=F32).astype(BF16)

    blocks = [block(s) for s in range(zs)]
    here = {0: blocks[0]}
    shards = lax.optimization_barrier((w_gate[0], w_up[0], w_down[0], blocks[7]))[:3]
    weights = lax.all_gather(jnp.concatenate(shards, 1), "dp", axis=0, tiled=True)

    def round_of(sends, steps, *more):
        outs = []
        if steps:
            stacked = [here[s].reshape(2, 2, capacity, width) for s in steps]
            same = jnp.concatenate([v[0, part] for part in range(2) for v in stacked], 0)
            cross = jnp.concatenate([v[1, part] for part in range(2) for v in stacked], 0)
            outs = [same] + [
                moved(same, lambda i: to_mate(i, xs)),
                moved(cross, lambda i: to_other(i, xs)),
                moved(cross, lambda i: to_diagonal(i, xs)),
            ]
        spread = len(outs)
        for s in sends:
            outs.append(moved(blocks[s], lambda i, s=s: along_z(i, s, zs, xs)))
        names = [s for s in (0, 2, 6, 3, 5, 4) if s not in here]
        rest = [blocks[s] for s in names if s not in sends]
        done = lax.optimization_barrier(tuple(outs + rest) + more)
        if steps:
            parts.append(done[:spread])
        for s, v in zip(sends, done[spread:]):
            here[s] = v
        for s, v in zip([s for s in names if s not in sends], done[spread + len(sends):]):
            blocks[s] = v
        return done[len(done) - len(more):]

    rounds = [((1, 7), ()), ((2, 6), (1, 7)), ((3, 5), (2, 6, 0)), ((4,), (3, 5)), ((), (4,))]
    parts = []
    for sends, steps in rounds[:3]:
        round_of(sends, steps)

    def block_of(some):
        pieces = [g[origin] for origin in range(4) for g in some]
        return expert_block(pieces, weights, capacity)

    early = block_of(parts)
    early = round_of(*rounds[3], *early)
    early = tuple(early) + tuple(back_block(early[3], weights))
    early = round_of(*rounds[4], *early)

    def returned(back):
        return [
            moved(back[1], lambda i: to_mate(i, xs)),
            moved(back[2], lambda i: to_other(i, xs)),
            moved(back[3], lambda i: to_diagonal(i, xs)),
        ]

    def summed(back, came, steps):
        same = (back[0].astype(F32) + came[0].astype(F32)).astype(BF16)
        cross = (came[1].astype(F32) + came[2].astype(F32)).astype(BF16)
        for k, s in enumerate(steps):
            cut = slice(k * capacity, (k + 1) * capacity)
            homes[s] = jnp.concatenate([same[cut], cross[cut]], 0)

    def home(s):
        route = [
            (c * dev_count + i, (1 - c) * dev_count + along_z(i, -s, zs, xs))
            for c in range(2) for i in range(dev_count)
        ]
        return lax.ppermute(homes[s], ("pipe", "expert"), route)

    homes = {}
    late_steps = [s for r in rounds[3:] for s in r[1]]
    early_steps = [s for r in rounds[:3] for s in r[1]]
    late = block_of(parts[2:])
    hidden_late, *back_early = lax.optimization_barrier((late[2], *early[4:]))
    came = returned(back_early)
    rows_x, rows_dy, hidden, slopes = zip(early[:4], late)
    half = hidden[0].shape[1]
    terms = outer_terms(rows_x, rows_dy, slopes, (hidden[0], hidden_late))
    grads = lax.psum_scatter(terms, "dp", scatter_dimension=0, tiled=True)
    back_late = back_block(after(late[3], terms), weights)
    *came, b0, b1, b2, b3 = lax.optimization_barrier((*came, *back_late))
    summed(early[4:], came, early_steps)
    back_late = [b0, b1, b2, b3]
    came = returned(back_late)
    near = {s: home(s) for s in (2, 6)}
    came = list(lax.optimization_barrier((*came, near[2], near[6], *[homes[s] for s in (0, 1, 7)])))
    near = dict(zip((2, 6), came[3:5]))
    homes.update(zip((0, 1, 7), came[5:8]))
    summed(back_late, came[:3], late_steps)
    homes = {s: home(s) for s in (3, 5, 4, 1, 7, 0)} | near
    summed_rows = jnp.concatenate([homes[s] for s in range(zs)], 0)
    slots = jnp.arange(2 * zs * capacity, dtype=jnp.int32)
    combine = (slots[None, :] == other_column.astype(jnp.int32)[:, None]).astype(BF16)
    passed = jnp.dot(combine, summed_rows, preferred_element_type=F32).astype(BF16)
    passed, grads = lax.optimization_barrier((passed, grads))
    return (
        passed[None],
        grads[:, :half].astype(F32)[None],
        grads[:, half:2 * half].astype(F32)[None],
        grads[:, 2 * half:].astype(F32)[None],
    )


def solution(mesh):
    placed = (
        P("pipe", ("expert", "dp"), None),
        P("pipe", ("expert", "dp"), None),
        P("pipe", ("expert", "dp"), None),
        P("pipe", ("expert", "dp")),
        P("pipe", "dp", "expert"),
        P("pipe", "dp", "expert"),
        P("pipe", "dp", "expert"),
    )
    return jax.shard_map(
        local,
        mesh=mesh,
        in_specs=placed,
        out_specs=(
            P("pipe", ("expert", "dp"), None),
            P("pipe", "dp", "expert"),
            P("pipe", "dp", "expert"),
            P("pipe", "dp", "expert"),
        ),
        check_vma=False,
    )
```

```python
import functools

import jax
import jax.numpy as jnp
from jax import lax
from jax.experimental import pallas as pl
from jax.experimental.pallas import tpu as pltpu
from jax.sharding import PartitionSpec as P

F32, BF16 = jnp.float32, jnp.bfloat16
OUTER = (((0,), (0,)), ((), ()))
INNER = (((1,), (1,)), ((), ()))
VMEM_BYTES = 56 * 2**20


def along_z(i, step, zs, xs):
    return (i // xs + step) % zs * xs + i % xs


def to_mate(i, xs):
    return i ^ 1


def to_other(i, xs):
    x = i % xs
    return i - x + (x + (1 if x % 2 else -1)) % xs


def to_diagonal(i, xs):
    x = i % xs
    return i - x + (x + 2) % xs


def moved(block, place):
    return lax.ppermute(block, "expert", [(i, place(i)) for i in range(lax.axis_size("expert"))])


def after(value, *earlier):
    return lax.optimization_barrier((value,) + earlier)[0]


def activations(gate_pre, up_pre, d_hidden):
    sigmoid_gate = jax.nn.sigmoid(gate_pre)
    silu_gate = gate_pre * sigmoid_gate
    hidden = (silu_gate * up_pre).astype(BF16)
    d_up = (d_hidden * silu_gate).astype(BF16)
    d_gate = (d_hidden * up_pre * sigmoid_gate * (1.0 + gate_pre * (1.0 - sigmoid_gate))).astype(BF16)
    return hidden, d_gate, d_up


def expert_kernel(counts, capacity, *refs):
    pieces, refs = refs[:len(counts)], refs[len(counts):]
    weights, out_x, out_dy, hidden, slopes, flat_x, flat_dy, sums, held, arrived, loaded, kept = refs
    width, half = flat_x.shape[1], hidden.shape[1]
    halves, cut = 2, 1024
    wide = width // halves
    loads = [
        pltpu.make_async_copy(
            weights.at[pl.ds(c * cut, cut), :], held.at[pl.ds(c * cut, cut), :], loaded.at[c]
        )
        for c in range(width // cut)
    ]
    for h in range(halves):
        columns = pl.ds(h * wide, wide)
        at = 0
        for piece, count in zip(pieces, counts):
            rows = count * capacity
            for part, flat in enumerate((flat_x, flat_dy)):
                pltpu.make_async_copy(
                    piece.at[pl.ds(part * rows, rows), columns],
                    flat.at[pl.ds(at, rows), columns],
                    arrived.at[part, h],
                ).start()
            at += rows
        for c in range(h * wide // cut, (h + 1) * wide // cut):
            loads[c].start()
    sums[...] = jnp.zeros_like(sums)
    keeps = []
    for h in range(halves):
        columns = pl.ds(h * wide, wide)
        for part, (flat, out) in enumerate(((flat_x, out_x), (flat_dy, out_dy))):
            whole = flat.at[:, columns]
            pltpu.make_async_copy(whole, whole, arrived.at[part, h]).wait()
            keep = pltpu.make_async_copy(whole, out.at[:, columns], kept.at[part, h])
            keep.start()
            keeps.append(keep)
        for c in range(h * wide // cut, (h + 1) * wide // cut):
            loads[c].wait()
            here = pl.ds(c * cut, cut)
            x, dy = flat_x[:, here], flat_dy[:, here]
            sums[:, :2 * half] += jnp.dot(x, held[here, :2 * half], preferred_element_type=F32)
            sums[:, 2 * half:] += jnp.dot(dy, held[here, 2 * half:], preferred_element_type=F32)

    hidden[...], slopes[:, :half], slopes[:, half:] = activations(
        sums[:, :half], sums[:, half:2 * half], sums[:, 2 * half:]
    )
    for keep in keeps:
        keep.wait()


def expert_block(pieces, weights, capacity):
    counts = [p.shape[0] // (2 * capacity) for p in pieces]
    rows = sum(counts) * capacity
    width, half = weights.shape[0], weights.shape[1] // 3
    anywhere, whole = pl.BlockSpec(memory_space=pl.ANY), pl.BlockSpec()
    return pl.pallas_call(
        functools.partial(expert_kernel, counts, capacity),
        in_specs=[anywhere] * (len(pieces) + 1),
        out_specs=[anywhere, anywhere, whole, whole],
        out_shape=[
            jax.ShapeDtypeStruct((rows, width), BF16),
            jax.ShapeDtypeStruct((rows, width), BF16),
            jax.ShapeDtypeStruct((rows, half), BF16),
            jax.ShapeDtypeStruct((rows, 2 * half), BF16),
        ],
        scratch_shapes=[
            pltpu.VMEM((rows, width), BF16),
            pltpu.VMEM((rows, width), BF16),
            pltpu.VMEM((rows, 3 * half), F32),
            pltpu.VMEM(weights.shape, BF16),
            pltpu.SemaphoreType.DMA((2, 2)),
            pltpu.SemaphoreType.DMA((width // 1024,)),
            pltpu.SemaphoreType.DMA((2, 2)),
        ],
        compiler_params=pltpu.CompilerParams(vmem_limit_bytes=VMEM_BYTES),
        cost_estimate=pl.CostEstimate(
            flops=6 * rows * width * half, bytes_accessed=20 * 2**20, transcendentals=rows * half
        ),
    )(*pieces, weights)


def back_kernel(slopes, weights, *backs):
    value = lax.dot_general(slopes[...], weights[...], INNER, preferred_element_type=F32).astype(BF16)
    rows = slopes.shape[0] // 4
    for i, back in enumerate(backs):
        back[...] = value[i * rows:(i + 1) * rows]


def back_block(slopes, weights):
    rows, both = slopes.shape
    width, cut = weights.shape[0], 1024
    return pl.pallas_call(
        back_kernel,
        grid=(width // cut,),
        in_specs=[
            pl.BlockSpec((rows, both), lambda k: (0, 0)),
            pl.BlockSpec((cut, both), lambda k: (k, 0)),
        ],
        out_specs=[pl.BlockSpec((rows // 4, cut), lambda k: (0, k))] * 4,
        out_shape=[jax.ShapeDtypeStruct((rows // 4, width), BF16)] * 4,
        compiler_params=pltpu.CompilerParams(vmem_limit_bytes=VMEM_BYTES),
        cost_estimate=pl.CostEstimate(
            flops=2 * rows * width * both, bytes_accessed=9 * 2**20, transcendentals=0
        ),
    )(slopes, weights)


def outer_kernel(x_early, x_late, dy_early, dy_late, slopes_early, slopes_late, hidden_early, hidden_late, out):
    def joined(early, late):
        return jnp.concatenate([early[...], late[...]], 0)

    def product(rows, values):
        return lax.dot_general(rows, values, OUTER, preferred_element_type=F32).astype(BF16)

    both = slopes_early.shape[1]
    out[:, :both] = product(joined(x_early, x_late), joined(slopes_early, slopes_late))
    out[:, both:] = product(joined(dy_early, dy_late), joined(hidden_early, hidden_late))


def outer_terms(rows_x, rows_dy, slopes, hidden):
    width, cut = rows_x[0].shape[1], 512
    columns = slopes[0].shape[1] + hidden[0].shape[1]
    return pl.pallas_call(
        outer_kernel,
        grid=(width // cut,),
        in_specs=[pl.BlockSpec((v.shape[0], cut), lambda k: (0, k)) for v in (*rows_x, *rows_dy)]
        + [pl.BlockSpec(v.shape, lambda k: (0, 0)) for v in (*slopes, *hidden)],
        out_specs=pl.BlockSpec((cut, columns), lambda k: (k, 0)),
        out_shape=jax.ShapeDtypeStruct((width, columns), BF16),
        compiler_params=pltpu.CompilerParams(vmem_limit_bytes=VMEM_BYTES),
        cost_estimate=pl.CostEstimate(flops=0, bytes_accessed=0, transcendentals=0),
    )(*rows_x, *rows_dy, *slopes, *hidden)


def local(layer_input, out_grad, routes, gates, w_gate, w_up, w_down):
    dev_count = lax.axis_size("expert")
    xs, zs = 4, dev_count // 4
    tok_rows, width = layer_input.shape[1:]
    experts = dev_count // 2
    capacity = 2 * tok_rows // experts
    me = lax.axis_index("expert")
    my_z, my_pair = me // xs, me % xs // 2

    tokens = layer_input[0]
    scaled = (gates[0][:, None] * out_grad[0].astype(F32)).astype(BF16)
    target = routes[0, :, 0]
    onehot = (target[:, None] == jnp.arange(experts, dtype=jnp.int32)[None, :]).astype(jnp.int32)
    before = jnp.cumsum(onehot, axis=0) - onehot
    rank = jnp.sum(before * onehot, axis=1)
    step = (target // 2 - my_z) % zs
    side = (target % 2) ^ my_pair
    home_column = (step * 2 + side) * capacity + rank
    other_column = lax.ppermute(home_column.astype(F32), "pipe", [(0, 1), (1, 0)])
    both = jnp.concatenate([tokens, scaled], axis=0)
    row_x = (step * 2 + side) * 2 * capacity + rank
    row_of = jnp.concatenate([row_x, row_x + capacity], axis=0)
    block_rows = 4 * capacity

    def block(s):
        rows = jnp.arange(block_rows, dtype=jnp.int32) + s * block_rows
        pick = (rows[:, None] == row_of[None, :]).astype(BF16)
        return jnp.dot(pick, both, preferred_element_type=F32).astype(BF16)

    blocks = [block(s) for s in range(zs)]
    here = {0: blocks[0]}
    shards = lax.optimization_barrier((w_gate[0], w_up[0], w_down[0], blocks[7]))[:3]
    weights = lax.all_gather(jnp.concatenate(shards, 1), "dp", axis=0, tiled=True)

    def round_of(sends, steps, *more):
        outs = []
        if steps:
            stacked = [here[s].reshape(2, 2, capacity, width) for s in steps]
            same = jnp.concatenate([v[0, part] for part in range(2) for v in stacked], 0)
            cross = jnp.concatenate([v[1, part] for part in range(2) for v in stacked], 0)
            outs = [same] + [
                moved(same, lambda i: to_mate(i, xs)),
                moved(cross, lambda i: to_other(i, xs)),
                moved(cross, lambda i: to_diagonal(i, xs)),
            ]
        spread = len(outs)
        for s in sends:
            outs.append(moved(blocks[s], lambda i, s=s: along_z(i, s, zs, xs)))
        names = [s for s in (0, 2, 6, 3, 5, 4) if s not in here]
        rest = [blocks[s] for s in names if s not in sends]
        done = lax.optimization_barrier(tuple(outs + rest) + more)
        if steps:
            parts.append(done[:spread])
        for s, v in zip(sends, done[spread:]):
            here[s] = v
        for s, v in zip([s for s in names if s not in sends], done[spread + len(sends):]):
            blocks[s] = v
        return done[len(done) - len(more):]

    rounds = [((1, 7), ()), ((2, 6), (1, 7)), ((3, 5), (2, 6, 0)), ((4,), (3, 5)), ((), (4,))]
    parts = []
    for sends, steps in rounds[:3]:
        round_of(sends, steps)

    def block_of(some):
        pieces = [g[origin] for origin in range(4) for g in some]
        return expert_block(pieces, weights, capacity)

    early = block_of(parts)
    early = round_of(*rounds[3], *early)
    early = tuple(early) + tuple(back_block(early[3], weights))
    early = round_of(*rounds[4], *early)

    def returned(back):
        return [
            moved(back[1], lambda i: to_mate(i, xs)),
            moved(back[2], lambda i: to_other(i, xs)),
            moved(back[3], lambda i: to_diagonal(i, xs)),
        ]

    def summed(back, came, steps):
        same = (back[0].astype(F32) + came[0].astype(F32)).astype(BF16)
        cross = (came[1].astype(F32) + came[2].astype(F32)).astype(BF16)
        for k, s in enumerate(steps):
            cut = slice(k * capacity, (k + 1) * capacity)
            homes[s] = jnp.concatenate([same[cut], cross[cut]], 0)

    def home(s):
        route = [
            (c * dev_count + i, (1 - c) * dev_count + along_z(i, -s, zs, xs))
            for c in range(2) for i in range(dev_count)
        ]
        return lax.ppermute(homes[s], ("pipe", "expert"), route)

    homes = {}
    late_steps = [s for r in rounds[3:] for s in r[1]]
    early_steps = [s for r in rounds[:3] for s in r[1]]
    late = block_of(parts[2:])
    hidden_late, *back_early = lax.optimization_barrier((late[2], *early[4:]))
    came = returned(back_early)
    rows_x, rows_dy, hidden, slopes = zip(early[:4], late)
    half = hidden[0].shape[1]
    terms = outer_terms(rows_x, rows_dy, slopes, (hidden[0], hidden_late))
    grads = lax.psum_scatter(terms, "dp", scatter_dimension=0, tiled=True)
    back_late = back_block(after(late[3], terms), weights)
    *came, b0, b1, b2, b3 = lax.optimization_barrier((*came, *back_late))
    summed(early[4:], came, early_steps)
    back_late = [b0, b1, b2, b3]
    came = returned(back_late)
    near_steps = (2, 6, 1, 7)
    near = [home(s) for s in near_steps]
    *came, rows_here = lax.optimization_barrier((*came, *near, homes[0]))
    near = dict(zip(near_steps, came[3:]))
    homes[0] = rows_here
    summed(back_late, came[:3], late_steps)
    homes = {s: home(s) for s in (4, 3, 5, 0)} | near
    summed_rows = jnp.concatenate([homes[s] for s in range(zs)], 0)
    slots = jnp.arange(2 * zs * capacity, dtype=jnp.int32)
    combine = (slots[None, :] == other_column.astype(jnp.int32)[:, None]).astype(BF16)
    passed = jnp.dot(combine, summed_rows, preferred_element_type=F32).astype(BF16)
    passed, grads = lax.optimization_barrier((passed, grads))
    return (
        passed[None],
        grads[:, :half].astype(F32)[None],
        grads[:, half:2 * half].astype(F32)[None],
        grads[:, 2 * half:].astype(F32)[None],
    )


def solution(mesh):
    placed = (
        P("pipe", ("expert", "dp"), None),
        P("pipe", ("expert", "dp"), None),
        P("pipe", ("expert", "dp"), None),
        P("pipe", ("expert", "dp")),
        P("pipe", "dp", "expert"),
        P("pipe", "dp", "expert"),
        P("pipe", "dp", "expert"),
    )
    return jax.shard_map(
        local,
        mesh=mesh,
        in_specs=placed,
        out_specs=(
            P("pipe", ("expert", "dp"), None),
            P("pipe", "dp", "expert"),
            P("pipe", "dp", "expert"),
            P("pipe", "dp", "expert"),
        ),
        check_vma=False,
    )
```
